32 devices in a mesh: dp: 8 (over z, x), space: 4 (over y, core).
Axes of the slice: x: 2, y: 2, z: 4, core: 2. Of those that a mesh axis runs over, the one named last changes fastest.
Arguments:
- volume: bfloat16 [8, 4, 16, 8, 512], P('dp', None, 'space'), may hold values from -6 to 6
- cotangent: bfloat16 [8, 32, 4, 2, 128], P('dp', None, 'space'), may hold values from -1 to 1
- w_first: bfloat16 [16, 4, 3, 3, 3], replicated, may hold values from -0.625 to 0.625
- b_first: float32 [16], replicated, may hold values from -3 to 3
- w_second: bfloat16 [32, 16, 3, 3, 3], replicated, may hold values from -0.3125 to 0.3125
- b_second: float32 [32], replicated, may hold values from -3 to 3
Outputs:
- output: bfloat16 [8, 32, 4, 2, 128], P('dp', None, 'space')
- grad_w_first: float32 [16, 4, 3, 3, 3], replicated
- grad_b_first: float32 [16], replicated
- grad_w_second: float32 [32, 16, 3, 3, 3], replicated
- grad_b_second: float32 [32], replicated
The draws below stay inside these ranges and needn't reach their ends.
All inputs are finite; a program needn't handle non-finite values.
Results may differ from the reference program's by a relative error of at most 0.0047.
Values may be sent and summed in bfloat16 or wider, within the bound.
A program may use at most 128 MiB of HBM per device.

```python
import math
import jax
import jax.numpy as jnp
from jax import lax

C0 = 4
C1 = 16
C2 = 32
Y = 8
Z = 512
X = 16
B = 8


def draw_cotangent(key, part):
    shape = (B, C2, X // 4, Y // 4, Z // 4)
    total = B * X * Y * Z
    base = 80.0 / math.sqrt(total)
    layer = jnp.arange(X // 4, dtype=jnp.float32) / max(X // 4 - 1, 1)
    rising = (3.0 ** layer)[None, None, :, None, None]
    sample = jnp.arange(B, dtype=jnp.float32) / max(B - 1, 1)
    sample_scale = (2.0 ** sample)[:, None, None, None, None]
    values = jax.random.normal(key, shape, jnp.float32)
    return jnp.clip(values * base * rising * sample_scale, -1.0, 1.0).astype(jnp.bfloat16)


def levels(key, dims, shards, smallest, top_value):
    loudness, own = 1.0, jax.random.fold_in(key, 6)
    for position, shards_of in shards:
        heights = jnp.exp(jax.random.uniform(jax.random.fold_in(own, position), (shards_of,), jnp.float32, smallest / len(shards), top_value / len(shards)))
        loudness = loudness * jnp.repeat(heights, dims[position] // shards_of).reshape([-1 if axis == position else 1 for axis in range(len(dims))])
    return loudness


def scatter_about(own_key, shape, scale, reach, cuts=(), kind=jnp.bfloat16):
    entries = scale * jax.random.normal(own_key, shape, jnp.float32)
    if cuts:
        entries = entries * levels(own_key, shape, cuts, -0.22, 0.18)
    return jnp.clip(entries, -reach, reach).astype(kind)


def setup_inputs(seed: int = 0) -> dict:
    arg_keys = jax.random.split(jax.random.key(seed), 7)
    return {
        "volume": scatter_about(arg_keys[0], (B, C0, X, Y, Z), 1.0, 6.0, ((0, 8), (2, 4))),
        "cotangent": draw_cotangent(jax.random.fold_in(arg_keys[6], 71), 0),
        "w_first": scatter_about(arg_keys[2], (C1, C0, 3, 3, 3), (C0 * 27) ** -0.5, 0.625),
        "b_first": scatter_about(arg_keys[3], (C1,), 0.5, 3.0, (), jnp.float32),
        "w_second": scatter_about(arg_keys[4], (C2, C1, 3, 3, 3), (C1 * 27) ** -0.5, 0.3125),
        "b_second": scatter_about(arg_keys[5], (C2,), 0.5, 3.0, (), jnp.float32),
    }


def conv_valid(inp, kern):
    return lax.conv_general_dilated(inp[None], kern, (1, 1, 1), 'VALID', dimension_numbers=('NCDHW', 'OIDHW', 'NCDHW'), precision=lax.Precision.HIGHEST, preferred_element_type=jnp.float32)[0]

def pad_all(field):
    return jnp.pad(field, ((0, 0), (1, 1), (1, 1), (1, 1)))

def avg_pool(field):
    chan, depth, height, width = field.shape
    return field.reshape(chan, depth // 2, 2, height // 2, 2, width // 2, 2).mean(axis=(2, 4, 6))

def upsample(field):
    return jnp.repeat(jnp.repeat(jnp.repeat(field, 2, axis=1), 2, axis=2), 2, axis=3)

def silu_slope(value):
    sig = jax.nn.sigmoid(value)
    return sig * (1.0 + value * (1.0 - sig))

def weight_grad(padded, grads):
    depth, height, width = grads.shape[1:]
    taps = []
    for depth_at in range(3):
        for row_at in range(3):
            for col_at in range(3):
                piece = padded[:, depth_at:depth_at + depth, row_at:row_at + height, col_at:col_at + width]
                taps.append(jnp.einsum('oxyz,cxyz->oc', grads, piece, precision=lax.Precision.HIGHEST))
    stacked = jnp.stack(taps, axis=-1)
    return stacked.reshape(grads.shape[0], padded.shape[0], 3, 3, 3)

def reference(volume, cotangent, w_first, b_first, w_second, b_second):
    kern_first = w_first.astype(jnp.float32)
    kern_second = w_second.astype(jnp.float32)
    flipped = jnp.transpose(jnp.flip(kern_second, (2, 3, 4)), (1, 0, 2, 3, 4))

    def one_sample(pair):
        sample, cot = pair
        padded_input = pad_all(sample.astype(jnp.float32))
        pre_first = conv_valid(padded_input, kern_first) + b_first[:, None, None, None]
        pooled = avg_pool(jax.nn.silu(pre_first)).astype(jnp.bfloat16)
        pooled = lax.optimization_barrier(pooled)
        padded_pool = pad_all(pooled.astype(jnp.float32))
        pre_second = conv_valid(padded_pool, kern_second) + b_second[:, None, None, None]
        output = avg_pool(jax.nn.silu(pre_second)).astype(jnp.bfloat16)
        grad_second = (upsample(cot.astype(jnp.float32)) * 0.125 * silu_slope(pre_second)).astype(jnp.bfloat16)
        grad_second = lax.optimization_barrier(grad_second).astype(jnp.float32)
        grad_w2 = weight_grad(padded_pool, grad_second)
        grad_b2 = lax.optimization_barrier(jnp.sum(grad_second, axis=(1, 2, 3)))
        back = conv_valid(pad_all(grad_second), flipped)
        grad_first = (upsample(back) * 0.125 * silu_slope(pre_first)).astype(jnp.bfloat16)
        grad_first = lax.optimization_barrier(grad_first).astype(jnp.float32)
        grad_w1 = weight_grad(padded_input, grad_first)
        grad_b1 = lax.optimization_barrier(jnp.sum(grad_first, axis=(1, 2, 3)))
        return (output, grad_w1, grad_b1, grad_w2, grad_b2)
    results = lax.map(one_sample, (volume, cotangent))
    return (results[0], lax.optimization_barrier(jnp.sum(results[1], axis=0)), lax.optimization_barrier(jnp.sum(results[2], axis=0)), lax.optimization_barrier(jnp.sum(results[3], axis=0)), lax.optimization_barrier(jnp.sum(results[4], axis=0)))
```

```python
import functools

import jax
import jax.numpy as jnp
import ml_dtypes
import numpy as np
from jax import lax
from jax.experimental import pallas as pl
from jax.experimental.pallas import tpu as pltpu
from jax.sharding import PartitionSpec as P

F32, BF16 = jnp.float32, jnp.bfloat16
MESH = pl.DeviceIdType.MESH
TILES = 16
EARLY = 14


def dot(a, b, over=(1, 0)):
    return lax.dot_general(a, b, (((over[0],), (over[1],)), ((), ())), preferred_element_type=F32)


def sigmoid(v):
    return 0.5 * jnp.tanh(0.5 * v) + 0.5


def lanes(rows, width=128):
    return lax.broadcasted_iota(jnp.int32, (rows, width), 1)


def column(row, n):
    at = lax.broadcasted_iota(jnp.int32, (n, n), 0)
    return jnp.sum(jnp.where(at == lanes(n, n), row, 0.0), axis=1, keepdims=True)


def as_row(col, n):
    at = lax.broadcasted_iota(jnp.int32, (n, 128), 0)
    return jnp.sum(jnp.where(at == lanes(n), col, 0.0), axis=0, keepdims=True)


def spread(plane, ch, dst, base):
    lane = lanes(ch)
    zero = jnp.zeros((ch, 128), F32)
    src = {}
    for row in range(2):
        for u in range(2):
            for col in range(2):
                at = (row * 2 + col) * ch
                src[row, u, col] = plane[at : at + ch, u * 128 : u * 128 + 128].astype(F32)
            src[row, u, -1] = jnp.where(lane == 0, 0.0, pltpu.roll(src[row, u, 1], 1, 1))
            src[row, u, 2] = jnp.where(lane == 127, 0.0, pltpu.roll(src[row, u, 0], 127, 1))
    for row in range(-1, 3):
        for col in range(-1, 3):
            at = base + ((row + 1) * 4 + col + 1) * ch
            if row == -1:
                pair = (zero, src[1, 0, col])
            elif row == 2:
                pair = (src[0, 1, col], zero)
            else:
                pair = (src[row, 0, col], src[row, 1, col])
            dst[at : at + ch, 0:128] = pair[0].astype(BF16)
            dst[at : at + ch, 128:256] = pair[1].astype(BF16)


def kernel(
    nd, ns,
    vol, cot, w1, b1, w2, b2, pmat, emat, rep1, rep2, operm,
    out, gw2, gw1, gb,
    field, slope1, taps, w1t, w2t, wback, pool, poolx, phalo, grad, gradx, ghalo, fold_a, fold_b,
    sums, parts, total,
    send_sem, recv_sem, s_send, s_recv, t_send, t_recv,
):
    dp, sp = lax.axis_index("dp"), lax.axis_index("space")
    count = nd * ns
    me = dp * ns + sp
    stride = count // TILES
    has_left, has_right = sp > 0, sp < ns - 1

    def device(index):
        return (index // ns, lax.rem(index, ns))

    barrier = pltpu.get_barrier_semaphore()

    def greet(k, carry):
        pl.semaphore_signal(barrier, inc=1, device_id=device(lax.rem(me + k, count)), device_id_type=MESH)
        return carry

    lax.fori_loop(1, count, greet, 0)

    class Exchange:
        def __init__(self, slot, to_left, to_right, from_left, from_right):
            self.left = lambda: pltpu.make_async_remote_copy(
                src_ref=to_left, dst_ref=from_right, send_sem=send_sem.at[2 * slot],
                recv_sem=recv_sem.at[2 * slot], device_id=(dp, sp - 1), device_id_type=MESH)
            self.right = lambda: pltpu.make_async_remote_copy(
                src_ref=to_right, dst_ref=from_left, send_sem=send_sem.at[2 * slot + 1],
                recv_sem=recv_sem.at[2 * slot + 1], device_id=(dp, sp + 1), device_id_type=MESH)
            self.from_left, self.from_right = from_left, from_right

        def start(self):
            @pl.when(has_left)
            def _():
                self.left().start()

            @pl.when(has_right)
            def _():
                self.right().start()

        def receive(self):
            @pl.when(has_left)
            def _():
                self.right().wait_recv()

            @pl.when(has_right)
            def _():
                self.left().wait_recv()

        def clear(self):
            @pl.when(jnp.logical_not(has_left))
            def _():
                self.from_left[...] = jnp.zeros(self.from_left.shape, BF16)

            @pl.when(jnp.logical_not(has_right))
            def _():
                self.from_right[...] = jnp.zeros(self.from_right.shape, BF16)

        def finish(self):
            @pl.when(has_left)
            def _():
                self.left().wait_send()

            @pl.when(has_right)
            def _():
                self.right().wait_send()

    rows = lambda ref, at, n: ref.at[pl.ds(at, n)]
    ex_field = Exchange(0, rows(field, 144, 144), rows(field, 576, 144), rows(field, 0, 144), rows(field, 720, 144))
    ex_pool = Exchange(1, rows(pool, 0, 64), rows(pool, 64, 64), rows(phalo, 0, 64), rows(phalo, 64, 64))
    ex_grad = Exchange(2, rows(grad, 0, 128), rows(grad, 128, 128), rows(ghalo, 0, 128), rows(ghalo, 128, 128))

    phases = dot(vol[...], pmat[...])
    part = [phases[:, q * 128 : q * 128 + 128] for q in range(4)]
    lane = lanes(128)
    before = jnp.where(lane == 0, 0.0, pltpu.roll(part[3], 1, 1))
    after = jnp.where(lane == 127, 0.0, pltpu.roll(part[0], 127, 1))
    part = [before] + part + [after]
    stacked = jnp.concatenate(
        [
            jnp.concatenate(
                [part[q][(c * 4 + x) * 8 : (c * 4 + x) * 8 + 8] for q in range(6) for c in range(4)], axis=0)
            for x in range(4)
        ],
        axis=1,
    ).astype(BF16)
    blocks = dot(emat[...], stacked).astype(BF16)
    for x in range(4):
        for u in range(2):
            field[144 * (x + 1) : 144 * (x + 2), u * 128 : u * 128 + 128] = blocks[
                u * 144 : u * 144 + 144, x * 128 : x * 128 + 128]

    pl.semaphore_wait(barrier, count - 1)
    ex_field.start()
    ex_field.clear()
    ex_pool.clear()
    ex_grad.clear()

    wide = lanes(24, 256)
    rep = dot(w1[...], rep1[...])
    taps[...] = jnp.zeros(taps.shape, F32)
    for q in range(4):
        for k in range(9):
            taps[q, k, 4 * q : 4 * q + 12, :] = rep[16 * k : 16 * k + 12]
    in_q = [lax.rem(wide // 16, 4) == q for q in range(4)]
    in_r = [wide // 64 == r for r in range(4)]
    band = []
    for k in range(9):
        blk = taps[0, k]
        for q in range(1, 4):
            blk = jnp.where(in_q[q], taps[q, k], blk)
        band.append(blk)
    rows_out = []
    for a in range(3):
        for y in range(6):
            blk = jnp.zeros((24, 256), F32)
            for r in range(4):
                if 0 <= y - r <= 2:
                    blk = jnp.where(in_r[r], band[a * 3 + y - r], blk)
            rows_out.append(blk)
    w1t[...] = jnp.concatenate(rows_out, axis=0).T.astype(BF16)

    bias1 = jnp.concatenate([column(b1[...], 16)] * 16, axis=0)
    bias2 = jnp.concatenate([column(b2[...], 32)] * 8, axis=0)
    acts = {}

    def first(i):
        v = dot(w1t[...], field[144 * i : 144 * i + 432]) + bias1
        s = sigmoid(v)
        slope1[256 * i : 256 * i + 256] = 0.125 * (s * (1.0 + v * (1.0 - s)))
        acts[i] = v * s

    first(1)
    first(2)

    rep = dot(w2[...], rep2[...])
    tap = lambda a, b, e: rep[((a * 3 + b) * 3 + e) * 16 : ((a * 3 + b) * 3 + e) * 16 + 16]
    own = lanes(16, 256) // 32
    rows_out = []
    for pi in range(4):
        for pr in range(4):
            for pq in range(4):
                blk = jnp.zeros((16, 256), F32)
                for k in range(8):
                    a, b, e = pi - k // 4, pr - (k // 2) % 2, pq - k % 2
                    if 0 <= a <= 2 and 0 <= b <= 2 and 0 <= e <= 2:
                        blk = jnp.where(own == k, tap(a, b, e), blk)
                rows_out.append(blk)
    w2t[...] = jnp.concatenate(rows_out, axis=0).T.astype(BF16)
    quarter = lanes(16) // 32
    back_tap = {}
    for a in range(3):
        for b in range(3):
            for col in range(2):
                blk = jnp.zeros((16, 128), F32)
                for e in range(3):
                    blk = jnp.where(quarter == col + 2 - e, tap(a, b, e)[:, 0:128], blk)
                back_tap[a, b, col] = blk.astype(BF16)
    none = jnp.zeros((16, 128), BF16)
    for k in range(8):
        for pi in range(4):
            for pr in range(4):
                at = (pi * 4 + pr) * 128
                wback[16 * k : 16 * k + 16, at : at + 128] = back_tap.get(
                    (k // 4 + 2 - pi, (k // 2) % 2 + 2 - pr, k % 2), none)

    ex_field.receive()
    first(0)
    first(3)
    for i in range(2):
        both = acts[2 * i] + acts[2 * i + 1]
        for row in range(2):
            for col in range(2):
                blk = 0.0
                for r in range(2 * row, 2 * row + 2):
                    for q in range(2 * col, 2 * col + 2):
                        blk = blk + both[(r * 4 + q) * 16 : (r * 4 + q) * 16 + 16]
                at = 64 * i + (row * 2 + col) * 16
                pool[at : at + 16] = (blk * 0.125).astype(BF16)
    ex_pool.start()
    spread(pool[0:64], 16, poolx, 256)
    spread(pool[64:128], 16, poolx, 512)
    v = dot(w2t[:, 256:768], poolx[256:768])
    cot_cols = dot(operm[...], cot[...])
    cot_cols = jnp.concatenate([cot_cols[0:32], cot_cols[32:64]], axis=1) * 0.125
    ex_pool.receive()
    spread(phalo[0:64], 16, poolx, 0)
    spread(phalo[64:128], 16, poolx, 768)
    v = v + dot(w2t[:, 0:256], poolx[0:256]) + dot(w2t[:, 768:1024], poolx[768:1024]) + bias2
    s = sigmoid(v)
    act = v * s
    slope = s * (1.0 + v * (1.0 - s))
    out_sum, grad_sum = 0.0, 0.0
    for k in range(8):
        blk = (cot_cols * slope[32 * k : 32 * k + 32]).astype(BF16)
        grad[32 * k : 32 * k + 32] = blk
        grad_sum = grad_sum + blk.astype(F32)
        out_sum = out_sum + act[32 * k : 32 * k + 32]
    ex_grad.start()

    prod = dot(poolx[...], grad[...], (1, 1))
    packed = [jnp.zeros((16, 128), F32) for _ in range(7)]
    for a in range(3):
        for b in range(3):
            for e in range(3):
                blk = jnp.zeros((16, 256), F32)
                for k in range(8):
                    at = (((k // 4 + a) * 4 + (k // 2) % 2 + b) * 4 + k % 2 + e) * 16
                    blk = jnp.where(own == k, prod[at : at + 16], blk)
                half = blk[:, 0:128] + blk[:, 128:256]
                half = half + pltpu.roll(half, 64, 1)
                half = half + pltpu.roll(half, 32, 1)
                at = (a * 3 + b) * 3 + e
                packed[at % 7] = jnp.where(quarter == at // 7, half, packed[at % 7])
    for j in range(7):
        sums[2 * j] = packed[j][0:8]
        sums[2 * j + 1] = packed[j][8:16]

    mine = lax.div(me, stride)
    owner = lax.rem(me, stride) == 0
    early = jnp.logical_and(owner, mine < EARLY)
    late = jnp.logical_and(owner, mine >= EARLY)

    def part_copy(j):
        return pltpu.make_async_remote_copy(
            src_ref=sums.at[j], dst_ref=parts.at[me], send_sem=s_send.at[j], recv_sem=s_recv,
            device_id=device(j * stride), device_id_type=MESH)

    def send_parts(low, high):
        def step(j, carry):
            @pl.when(j * stride != me)
            def _():
                part_copy(j).start()
            return carry

        lax.fori_loop(low, high, step, 0)

    def total_copy(to, sem):
        return pltpu.make_async_remote_copy(
            src_ref=total.at[mine], dst_ref=total.at[mine], send_sem=t_send, recv_sem=t_recv.at[sem],
            device_id=device(to), device_id_type=MESH)

    def add_up(sem):
        pltpu.make_async_copy(parts.at[pl.ds(0, count - 1)], parts.at[pl.ds(0, count - 1)], s_recv).wait()
        parts[me] = sums[mine]
        total[mine] = jnp.sum(parts[...], axis=0)

        def step(k, carry):
            total_copy(lax.rem(me + k, count), sem).start()
            return carry

        lax.fori_loop(1, count, step, 0)

    def take(sem, tiles, is_mine):
        def wait(n):
            pltpu.make_async_copy(total.at[pl.ds(0, n)], total.at[pl.ds(0, n)], t_recv.at[sem]).wait()

        @pl.when(is_mine)
        def _():
            wait(tiles - 1)

        @pl.when(jnp.logical_not(is_mine))
        def _():
            wait(tiles)

    send_parts(0, EARLY)

    res = (out_sum * 0.125).astype(BF16)
    res = jnp.concatenate([res[:, 0:128], res[:, 128:256]], axis=0)
    out[...] = dot(operm[...], res, (0, 0)).astype(BF16)

    spread(grad[0:128], 32, gradx, 512)
    spread(grad[128:256], 32, gradx, 1024)
    back = dot(wback[:, 512:1536], gradx[512:1536])
    ex_grad.receive()
    spread(ghalo[0:128], 32, gradx, 0)
    spread(ghalo[128:256], 32, gradx, 1536)
    back = back + dot(wback[:, 0:512], gradx[0:512]) + dot(wback[:, 1536:2048], gradx[1536:2048])

    prod = jnp.zeros((432, 256), F32)
    bias_sum = jnp.zeros((16, 256), F32)
    for i in range(4):
        blks = []
        for r in range(4):
            for q in range(4):
                at = (((i // 2) * 2 + r // 2) * 2 + q // 2) * 16
                k = 256 * i + (r * 4 + q) * 16
                blk = (back[at : at + 16] * slope1[k : k + 16]).astype(BF16)
                bias_sum = bias_sum + blk.astype(F32)
                blks.append(blk)
        prod = prod + dot(field[144 * i : 144 * i + 432], jnp.concatenate(blks, axis=0), (1, 1))

    for a in range(3):
        for b in range(3):
            blk = jnp.zeros((24, 256), F32)
            for r in range(4):
                at = (a * 6 + r + b) * 24
                blk = jnp.where(in_r[r], prod[at : at + 24], blk)
            half = blk[:, 0:128] + blk[:, 128:256]
            fold_a[a * 3 + b] = half + pltpu.roll(half, 64, 1)
    sixteenth = lanes(12) // 16
    for k in range(9):
        blk = jnp.zeros((12, 128), F32)
        for q in range(4):
            blk = jnp.where(lax.rem(sixteenth, 4) == q, fold_a[k, 4 * q : 4 * q + 12, :], blk)
        blk = blk + pltpu.roll(blk, 32, 1)
        blk = blk + pltpu.roll(blk, 16, 1)
        fold_b[12 * k : 12 * k + 12, :] = blk
    fold_b[108:120, :] = jnp.zeros((12, 128), F32)
    blk = fold_b[0:16]
    for g in range(1, 8):
        blk = jnp.where(lanes(16) // 16 == g, fold_b[14 * g : 14 * g + 16, :], blk)
    at = lax.broadcasted_iota(jnp.int32, (16, 128), 0)
    row1 = as_row(jnp.sum(bias_sum, axis=1, keepdims=True), 16)
    row2 = as_row(jnp.sum(grad_sum, axis=1, keepdims=True), 32)
    blk = jnp.where(at == 14, row1, jnp.where(at == 15, row2, blk))
    sums[EARLY] = blk[0:8]
    sums[EARLY + 1] = blk[8:16]
    send_parts(EARLY, TILES)

    @pl.when(early)
    def _():
        add_up(0)

    @pl.when(late)
    def _():
        add_up(1)

    take(0, EARLY, early)
    for g in range(4):
        n = 112 if g < 3 else 96
        blk = total[0 : n // 8].reshape(n, 128)
        if g:
            blk = pltpu.roll(blk, 128 - 32 * g, 1)
        gw2[112 * g : 112 * g + n] = blk[:, 0:32]
    take(1, TILES - EARLY, late)
    blk = jnp.concatenate([total[EARLY], total[EARLY + 1]], axis=0)
    gb[...] = total[EARLY + 1]
    for g in range(8):
        n = 14 if g < 7 else 10
        turned = pltpu.roll(blk, 128 - 16 * g, 1) if g else blk
        gw1[14 * g : 14 * g + n] = turned[0:n, 0:16]

    ex_field.finish()
    ex_pool.finish()
    ex_grad.finish()

    def sent(j, carry):
        @pl.when(j * stride != me)
        def _():
            part_copy(j).wait_send()
        return carry

    lax.fori_loop(0, TILES, sent, 0)

    @pl.when(owner)
    def _():
        pltpu.make_async_copy(parts.at[pl.ds(0, count - 1)], parts.at[pl.ds(0, count - 1)], t_send).wait()


def tables():
    pmat = np.zeros((512, 512), np.float32)
    for z in range(512):
        pmat[z, (z % 4) * 128 + z // 4] = 1
    emat = np.zeros((2, 6, 6, 4, 6, 4, 8), np.float32)
    for u in range(2):
        for yr in range(6):
            y = 4 * u + yr - 1
            if 0 <= y < 8:
                for q in range(6):
                    for c in range(4):
                        emat[u, yr, q, c, q, c, y] = 1
    rep1 = np.tile(np.eye(16, dtype=np.float32), (1, 16))
    rep2 = np.tile(np.eye(32, dtype=np.float32), (1, 8))
    operm = np.zeros((64, 64), np.float32)
    for u in range(2):
        for o in range(32):
            operm[u * 32 + o, o * 2 + u] = 1
    return [t.astype(ml_dtypes.bfloat16) for t in (pmat, emat.reshape(288, 192), rep1, rep2, operm)]


def shards(nd, ns, volume, cotangent, w_first, b_first, w_second, b_second):
    count = nd * ns
    w1 = jnp.transpose(w_first, (2, 3, 4, 1, 0)).reshape(9, 12, 16)
    w1 = jnp.pad(w1, ((0, 0), (0, 4), (0, 0))).reshape(144, 16)
    w2 = jnp.transpose(w_second, (2, 3, 4, 1, 0)).reshape(432, 32)
    vm = pl.BlockSpec(memory_space=pltpu.VMEM)
    dma = pltpu.SemaphoreType.DMA
    out, gw2, gw1, gb = pl.pallas_call(
        functools.partial(kernel, nd, ns),
        out_shape=[
            jax.ShapeDtypeStruct((64, 128), BF16),
            jax.ShapeDtypeStruct((432, 32), F32),
            jax.ShapeDtypeStruct((108, 16), F32),
            jax.ShapeDtypeStruct((8, 128), F32),
        ],
        in_specs=[vm] * 11,
        out_specs=[vm] * 4,
        scratch_shapes=[
            pltpu.VMEM((864, 256), BF16),
            pltpu.VMEM((1024, 256), F32),
            pltpu.VMEM((4, 9, 24, 256), F32),
            pltpu.VMEM((256, 432), BF16),
            pltpu.VMEM((256, 1024), BF16),
            pltpu.VMEM((128, 2048), BF16),
            pltpu.VMEM((128, 256), BF16),
            pltpu.VMEM((1024, 256), BF16),
            pltpu.VMEM((128, 256), BF16),
            pltpu.VMEM((256, 256), BF16),
            pltpu.VMEM((2048, 256), BF16),
            pltpu.VMEM((256, 256), BF16),
            pltpu.VMEM((9, 24, 128), F32),
            pltpu.VMEM((120, 128), F32),
            pltpu.VMEM((TILES, 8, 128), F32),
            pltpu.VMEM((count, 8, 128), F32),
            pltpu.VMEM((TILES, 8, 128), F32),
            dma((6,)),
            dma((6,)),
            dma((TILES,)),
            dma,
            dma,
            dma((2,)),
        ],
        compiler_params=pltpu.CompilerParams(
            collective_id=0, has_side_effects=True, vmem_limit_bytes=48 * 1024 * 1024),
        cost_estimate=pl.CostEstimate(flops=10**9, bytes_accessed=2 * 10**6, transcendentals=3 * 10**5),
    )(
        volume.reshape(128, 512), cotangent.reshape(64, 128), w1, b_first.reshape(1, 16), w2,
        b_second.reshape(1, 32), *tables(),
    )
    grad_w1 = jnp.transpose(gw1.reshape(3, 3, 3, 4, 16), (4, 3, 0, 1, 2))
    grad_w2 = jnp.transpose(gw2.reshape(3, 3, 3, 16, 32), (4, 3, 0, 1, 2))
    return out.reshape(1, 32, 1, 2, 128), grad_w1, gb[6, :16], grad_w2, gb[7, :32]


def solution(mesh):
    placed = (
        P("dp", None, "space", None, None),
        P("dp", None, "space", None, None),
        P(),
        P(),
        P(),
        P(),
    )
    return jax.shard_map(
        functools.partial(shards, mesh.shape["dp"], mesh.shape["space"]),
        mesh=mesh,
        in_specs=placed,
        out_specs=(P("dp", None, "space", None, None), P(), P(), P(), P()),
        check_vma=False,
    )
```

```python
import functools

import jax
import jax.numpy as jnp
import ml_dtypes
import numpy as np
from jax import lax
from jax.experimental import pallas as pl
from jax.experimental.pallas import tpu as pltpu
from jax.sharding import PartitionSpec as P

F32, BF16 = jnp.float32, jnp.bfloat16
MESH = pl.DeviceIdType.MESH
TILES = 16
INPUTS = 11
EARLY = 14


def dot(a, b, over=(1, 0)):
    return lax.dot_general(a, b, (((over[0],), (over[1],)), ((), ())), preferred_element_type=F32)


def sigmoid(v):
    return 0.5 * jnp.tanh(0.5 * v) + 0.5


def lanes(rows, width=128):
    return lax.broadcasted_iota(jnp.int32, (rows, width), 1)


def column(row, n):
    at = lax.broadcasted_iota(jnp.int32, (n, n), 0)
    return jnp.sum(jnp.where(at == lanes(n, n), row, 0.0), axis=1, keepdims=True)


def as_row(col, n):
    at = lax.broadcasted_iota(jnp.int32, (n, 128), 0)
    return jnp.sum(jnp.where(at == lanes(n), col, 0.0), axis=0, keepdims=True)


def spread(plane, ch, dst, base):
    lane = lanes(ch)
    zero = jnp.zeros((ch, 128), F32)
    src = {}
    for row in range(2):
        for u in range(2):
            for col in range(2):
                at = (row * 2 + col) * ch
                src[row, u, col] = plane[at : at + ch, u * 128 : u * 128 + 128].astype(F32)
            src[row, u, -1] = jnp.where(lane == 0, 0.0, pltpu.roll(src[row, u, 1], 1, 1))
            src[row, u, 2] = jnp.where(lane == 127, 0.0, pltpu.roll(src[row, u, 0], 127, 1))
    for row in range(-1, 3):
        for col in range(-1, 3):
            at = base + ((row + 1) * 4 + col + 1) * ch
            if row == -1:
                pair = (zero, src[1, 0, col])
            elif row == 2:
                pair = (src[0, 1, col], zero)
            else:
                pair = (src[row, 0, col], src[row, 1, col])
            dst[at : at + ch, 0:128] = pair[0].astype(BF16)
            dst[at : at + ch, 128:256] = pair[1].astype(BF16)


def kernel(
    nd, ns,
    *refs,
):
    hbm, (out, total) = refs[:INPUTS], refs[INPUTS : INPUTS + 2]
    held, refs = refs[INPUTS + 2 : 2 * INPUTS + 2], refs[2 * INPUTS + 2 :]
    vol, cot, w1, b1, w2, b2, pmat, emat, rep1, rep2, operm = held
    (
    field, slope1, taps, w1t, w2t, wback, pool, poolx, phalo, grad, gradx, ghalo, fold_a, fold_b,
    w1_rows, sums, parts, load_sem, send_sem, recv_sem, s_send, s_recv, t_send, t_recv,
    ) = refs
    loads = [pltpu.make_async_copy(hbm[i], held[i], load_sem.at[i]) for i in range(INPUTS)]
    for copy in loads:
        copy.start()
    dp, sp = lax.axis_index("dp"), lax.axis_index("space")
    count = nd * ns
    me = dp * ns + sp
    stride = count // TILES
    has_left, has_right = sp > 0, sp < ns - 1

    def device(index):
        return (index // ns, lax.rem(index, ns))

    barrier = pltpu.get_barrier_semaphore()

    def greet(k, carry):
        pl.semaphore_signal(barrier, inc=1, device_id=device(lax.rem(me + k, count)), device_id_type=MESH)
        return carry

    lax.fori_loop(1, count, greet, 0)

    class Exchange:
        def __init__(self, slot, to_left, to_right, from_left, from_right):
            self.left = lambda: pltpu.make_async_remote_copy(
                src_ref=to_left, dst_ref=from_right, send_sem=send_sem.at[2 * slot],
                recv_sem=recv_sem.at[2 * slot], device_id=(dp, sp - 1), device_id_type=MESH)
            self.right = lambda: pltpu.make_async_remote_copy(
                src_ref=to_right, dst_ref=from_left, send_sem=send_sem.at[2 * slot + 1],
                recv_sem=recv_sem.at[2 * slot + 1], device_id=(dp, sp + 1), device_id_type=MESH)
            self.from_left, self.from_right = from_left, from_right

        def start(self):
            @pl.when(has_left)
            def _():
                self.left().start()

            @pl.when(has_right)
            def _():
                self.right().start()

        def receive(self):
            @pl.when(has_left)
            def _():
                self.right().wait_recv()

            @pl.when(has_right)
            def _():
                self.left().wait_recv()

        def clear(self):
            @pl.when(jnp.logical_not(has_left))
            def _():
                self.from_left[...] = jnp.zeros(self.from_left.shape, BF16)

            @pl.when(jnp.logical_not(has_right))
            def _():
                self.from_right[...] = jnp.zeros(self.from_right.shape, BF16)

        def finish(self):
            @pl.when(has_left)
            def _():
                self.left().wait_send()

            @pl.when(has_right)
            def _():
                self.right().wait_send()

    rows = lambda ref, at, n: ref.at[pl.ds(at, n)]
    ex_field = Exchange(0, rows(field, 144, 144), rows(field, 576, 144), rows(field, 0, 144), rows(field, 720, 144))
    ex_pool = Exchange(1, rows(pool, 0, 64), rows(pool, 64, 64), rows(phalo, 0, 64), rows(phalo, 64, 64))
    ex_grad = Exchange(2, rows(grad, 0, 128), rows(grad, 128, 128), rows(ghalo, 0, 128), rows(ghalo, 128, 128))

    for copy in loads:
        copy.wait()
    phases = dot(vol[...], pmat[...])
    part = [phases[:, q * 128 : q * 128 + 128] for q in range(4)]
    lane = lanes(128)
    before = jnp.where(lane == 0, 0.0, pltpu.roll(part[3], 1, 1))
    after = jnp.where(lane == 127, 0.0, pltpu.roll(part[0], 127, 1))
    part = [before] + part + [after]
    stacked = jnp.concatenate(
        [
            jnp.concatenate(
                [part[q][(c * 4 + x) * 8 : (c * 4 + x) * 8 + 8] for q in range(6) for c in range(4)], axis=0)
            for x in range(4)
        ],
        axis=1,
    ).astype(BF16)
    blocks = dot(emat[...], stacked).astype(BF16)
    for x in range(4):
        for u in range(2):
            field[144 * (x + 1) : 144 * (x + 2), u * 128 : u * 128 + 128] = blocks[
                u * 144 : u * 144 + 144, x * 128 : x * 128 + 128]

    pl.semaphore_wait(barrier, count - 1)
    ex_field.start()
    ex_field.clear()
    ex_pool.clear()
    ex_grad.clear()

    wide = lanes(24, 256)
    w1_rows[...] = jnp.zeros(w1_rows.shape, F32)
    for k in range(27):
        at = 16 * (k // 3) + 4 * (k % 3)
        w1_rows[at : at + 4, :] = w1[k].astype(F32)
    rep = dot(w1_rows[...].astype(BF16), rep1[...])
    taps[...] = jnp.zeros(taps.shape, F32)
    for q in range(4):
        for k in range(9):
            taps[q, k, 4 * q : 4 * q + 12, :] = rep[16 * k : 16 * k + 12]
    in_q = [lax.rem(wide // 16, 4) == q for q in range(4)]
    in_r = [wide // 64 == r for r in range(4)]
    band = []
    for k in range(9):
        blk = taps[0, k]
        for q in range(1, 4):
            blk = jnp.where(in_q[q], taps[q, k], blk)
        band.append(blk)
    rows_out = []
    for a in range(3):
        for y in range(6):
            blk = jnp.zeros((24, 256), F32)
            for r in range(4):
                if 0 <= y - r <= 2:
                    blk = jnp.where(in_r[r], band[a * 3 + y - r], blk)
            rows_out.append(blk)
    w1t[...] = jnp.concatenate(rows_out, axis=0).T.astype(BF16)

    bias1 = jnp.concatenate([column(b1[...], 16)] * 16, axis=0)
    bias2 = jnp.concatenate([column(b2[...], 32)] * 8, axis=0)
    acts = {}

    def first(i):
        v = dot(w1t[...], field[144 * i : 144 * i + 432]) + bias1
        s = sigmoid(v)
        slope1[256 * i : 256 * i + 256] = 0.125 * (s * (1.0 + v * (1.0 - s)))
        acts[i] = v * s

    first(1)
    first(2)

    rep = dot(w2[...], rep2[...])
    tap = lambda a, b, e: rep[((a * 3 + b) * 3 + e) * 16 : ((a * 3 + b) * 3 + e) * 16 + 16]
    own = lanes(16, 256) // 32
    rows_out = []
    for pi in range(4):
        for pr in range(4):
            for pq in range(4):
                blk = jnp.zeros((16, 256), F32)
                for k in range(8):
                    a, b, e = pi - k // 4, pr - (k // 2) % 2, pq - k % 2
                    if 0 <= a <= 2 and 0 <= b <= 2 and 0 <= e <= 2:
                        blk = jnp.where(own == k, tap(a, b, e), blk)
                rows_out.append(blk)
    w2t[...] = jnp.concatenate(rows_out, axis=0).T.astype(BF16)
    quarter = lanes(16) // 32
    back_tap = {}
    for a in range(3):
        for b in range(3):
            for col in range(2):
                blk = jnp.zeros((16, 128), F32)
                for e in range(3):
                    blk = jnp.where(quarter == col + 2 - e, tap(a, b, e)[:, 0:128], blk)
                back_tap[a, b, col] = blk.astype(BF16)
    none = jnp.zeros((16, 128), BF16)
    for k in range(8):
        for pi in range(4):
            for pr in range(4):
                at = (pi * 4 + pr) * 128
                wback[16 * k : 16 * k + 16, at : at + 128] = back_tap.get(
                    (k // 4 + 2 - pi, (k // 2) % 2 + 2 - pr, k % 2), none)

    ex_field.receive()
    first(0)
    first(3)
    for i in range(2):
        both = acts[2 * i] + acts[2 * i + 1]
        for row in range(2):
            for col in range(2):
                blk = 0.0
                for r in range(2 * row, 2 * row + 2):
                    for q in range(2 * col, 2 * col + 2):
                        blk = blk + both[(r * 4 + q) * 16 : (r * 4 + q) * 16 + 16]
                at = 64 * i + (row * 2 + col) * 16
                pool[at : at + 16] = (blk * 0.125).astype(BF16)
    ex_pool.start()
    spread(pool[0:64], 16, poolx, 256)
    spread(pool[64:128], 16, poolx, 512)
    v = dot(w2t[:, 256:768], poolx[256:768])
    cot_cols = dot(operm[...], cot[...])
    cot_cols = jnp.concatenate([cot_cols[0:32], cot_cols[32:64]], axis=1) * 0.125
    ex_pool.receive()
    spread(phalo[0:64], 16, poolx, 0)
    spread(phalo[64:128], 16, poolx, 768)
    v = v + dot(w2t[:, 0:256], poolx[0:256]) + dot(w2t[:, 768:1024], poolx[768:1024]) + bias2
    s = sigmoid(v)
    act = v * s
    slope = s * (1.0 + v * (1.0 - s))
    out_sum, grad_sum = 0.0, 0.0
    for k in range(8):
        blk = (cot_cols * slope[32 * k : 32 * k + 32]).astype(BF16)
        grad[32 * k : 32 * k + 32] = blk
        grad_sum = grad_sum + blk.astype(F32)
        out_sum = out_sum + act[32 * k : 32 * k + 32]
    ex_grad.start()

    prod = dot(poolx[...], grad[...], (1, 1))
    packed = [jnp.zeros((16, 128), F32) for _ in range(7)]
    for a in range(3):
        for b in range(3):
            for e in range(3):
                blk = jnp.zeros((16, 256), F32)
                for k in range(8):
                    at = (((k // 4 + a) * 4 + (k // 2) % 2 + b) * 4 + k % 2 + e) * 16
                    blk = jnp.where(own == k, prod[at : at + 16], blk)
                half = blk[:, 0:128] + blk[:, 128:256]
                half = half + pltpu.roll(half, 64, 1)
                half = half + pltpu.roll(half, 32, 1)
                at = (a * 3 + b) * 3 + e
                packed[at % 7] = jnp.where(quarter == at // 7, half, packed[at % 7])
    for j in range(7):
        sums[2 * j] = packed[j][0:8]
        sums[2 * j + 1] = packed[j][8:16]

    mine = lax.div(me, stride)
    owner = lax.rem(me, stride) == 0
    early = jnp.logical_and(owner, mine < EARLY)
    late = jnp.logical_and(owner, mine >= EARLY)

    def part_copy(j):
        return pltpu.make_async_remote_copy(
            src_ref=sums.at[j], dst_ref=parts.at[me], send_sem=s_send.at[j], recv_sem=s_recv,
            device_id=device(j * stride), device_id_type=MESH)

    def send_parts(low, high):
        def step(j, carry):
            @pl.when(j * stride != me)
            def _():
                part_copy(j).start()
            return carry

        lax.fori_loop(low, high, step, 0)

    def total_copy(to, sem):
        return pltpu.make_async_remote_copy(
            src_ref=total.at[mine], dst_ref=total.at[mine], send_sem=t_send, recv_sem=t_recv.at[sem],
            device_id=device(to), device_id_type=MESH)

    def add_up(sem):
        pltpu.make_async_copy(parts.at[pl.ds(0, count - 1)], parts.at[pl.ds(0, count - 1)], s_recv).wait()
        parts[me] = sums[mine]
        total[mine] = jnp.sum(parts[...], axis=0)

        def step(k, carry):
            total_copy(lax.rem(me + k, count), sem).start()
            return carry

        lax.fori_loop(1, count, step, 0)

    def take(sem, tiles, is_mine):
        def wait(n):
            pltpu.make_async_copy(total.at[pl.ds(0, n)], total.at[pl.ds(0, n)], t_recv.at[sem]).wait()

        @pl.when(is_mine)
        def _():
            wait(tiles - 1)

        @pl.when(jnp.logical_not(is_mine))
        def _():
            wait(tiles)

    send_parts(0, EARLY)

    res = (out_sum * 0.125).astype(BF16)
    res = jnp.concatenate([res[:, 0:128], res[:, 128:256]], axis=0)
    out[...] = dot(operm[...], res, (0, 0)).astype(BF16)

    spread(grad[0:128], 32, gradx, 512)
    spread(grad[128:256], 32, gradx, 1024)
    back = dot(wback[:, 512:1536], gradx[512:1536])
    ex_grad.receive()
    spread(ghalo[0:128], 32, gradx, 0)
    spread(ghalo[128:256], 32, gradx, 1536)
    back = back + dot(wback[:, 0:512], gradx[0:512]) + dot(wback[:, 1536:2048], gradx[1536:2048])

    prod = jnp.zeros((432, 256), F32)
    bias_sum = jnp.zeros((16, 256), F32)
    for i in range(4):
        blks = []
        for r in range(4):
            for q in range(4):
                at = (((i // 2) * 2 + r // 2) * 2 + q // 2) * 16
                k = 256 * i + (r * 4 + q) * 16
                blk = (back[at : at + 16] * slope1[k : k + 16]).astype(BF16)
                bias_sum = bias_sum + blk.astype(F32)
                blks.append(blk)
        prod = prod + dot(field[144 * i : 144 * i + 432], jnp.concatenate(blks, axis=0), (1, 1))

    for a in range(3):
        for b in range(3):
            blk = jnp.zeros((24, 256), F32)
            for r in range(4):
                at = (a * 6 + r + b) * 24
                blk = jnp.where(in_r[r], prod[at : at + 24], blk)
            half = blk[:, 0:128] + blk[:, 128:256]
            fold_a[a * 3 + b] = half + pltpu.roll(half, 64, 1)
    sixteenth = lanes(12) // 16
    for k in range(9):
        blk = jnp.zeros((12, 128), F32)
        for q in range(4):
            blk = jnp.where(lax.rem(sixteenth, 4) == q, fold_a[k, 4 * q : 4 * q + 12, :], blk)
        blk = blk + pltpu.roll(blk, 32, 1)
        blk = blk + pltpu.roll(blk, 16, 1)
        fold_b[12 * k : 12 * k + 12, :] = blk
    fold_b[108:120, :] = jnp.zeros((12, 128), F32)
    blk = fold_b[0:16]
    for g in range(1, 8):
        blk = jnp.where(lanes(16) // 16 == g, fold_b[14 * g : 14 * g + 16, :], blk)
    at = lax.broadcasted_iota(jnp.int32, (16, 128), 0)
    row1 = as_row(jnp.sum(bias_sum, axis=1, keepdims=True), 16)
    row2 = as_row(jnp.sum(grad_sum, axis=1, keepdims=True), 32)
    blk = jnp.where(at == 14, row1, jnp.where(at == 15, row2, blk))
    sums[EARLY] = blk[0:8]
    sums[EARLY + 1] = blk[8:16]
    send_parts(EARLY, TILES)

    @pl.when(early)
    def _():
        add_up(0)

    @pl.when(late)
    def _():
        add_up(1)

    take(0, EARLY, early)
    take(1, TILES - EARLY, late)
    ex_field.finish()
    ex_pool.finish()
    ex_grad.finish()

    def sent(j, carry):
        @pl.when(j * stride != me)
        def _():
            part_copy(j).wait_send()
        return carry

    lax.fori_loop(0, TILES, sent, 0)

    @pl.when(owner)
    def _():
        pltpu.make_async_copy(parts.at[pl.ds(0, count - 1)], parts.at[pl.ds(0, count - 1)], t_send).wait()


def unpack(res, total, out, gw2, gw1, gb1, gb2, rows):
    out[...] = res[...]
    for g in range(4):
        n = 112 if g < 3 else 96
        blk = total[0 : n // 8].reshape(n, 128)
        if g:
            blk = pltpu.roll(blk, 128 - 32 * g, 1)
        gw2[112 * g : 112 * g + n] = blk[:, 0:32]
    blk = jnp.concatenate([total[EARLY], total[EARLY + 1]], axis=0)
    for g in range(8):
        n = 14 if g < 7 else 10
        turned = pltpu.roll(blk, 128 - 16 * g, 1) if g else blk
        rows[14 * g : 14 * g + n] = turned[0:n]
    for k in range(27):
        gw1[k] = rows[4 * k : 4 * k + 4, 0:16]
    gb1[...] = blk[14:15, 0:16]
    gb2[...] = blk[15:16, 0:32]


def tables():
    pmat = np.zeros((512, 512), np.float32)
    for z in range(512):
        pmat[z, (z % 4) * 128 + z // 4] = 1
    emat = np.zeros((2, 6, 6, 4, 6, 4, 8), np.float32)
    for u in range(2):
        for yr in range(6):
            y = 4 * u + yr - 1
            if 0 <= y < 8:
                for q in range(6):
                    for c in range(4):
                        emat[u, yr, q, c, q, c, y] = 1
    rep1 = np.tile(np.eye(16, dtype=np.float32), (1, 16))
    rep2 = np.tile(np.eye(32, dtype=np.float32), (1, 8))
    operm = np.zeros((64, 64), np.float32)
    for u in range(2):
        for o in range(32):
            operm[u * 32 + o, o * 2 + u] = 1
    return [t.astype(ml_dtypes.bfloat16) for t in (pmat, emat.reshape(288, 192), rep1, rep2, operm)]


def shards(nd, ns, volume, cotangent, w_first, b_first, w_second, b_second):
    count = nd * ns
    w1 = jnp.transpose(w_first, (2, 3, 4, 1, 0)).reshape(27, 4, 16)
    w2 = jnp.transpose(w_second, (2, 3, 4, 1, 0)).reshape(432, 32)
    vm = pl.BlockSpec(memory_space=pltpu.VMEM)
    dma = pltpu.SemaphoreType.DMA
    operands = [
        volume.reshape(128, 512), cotangent.reshape(64, 128), w1, b_first.reshape(1, 16), w2,
        b_second.reshape(1, 32), *tables(),
    ]
    out, total = pl.pallas_call(
        functools.partial(kernel, nd, ns),
        out_shape=[
            jax.ShapeDtypeStruct((64, 128), BF16),
            jax.ShapeDtypeStruct((TILES, 8, 128), F32),
        ],
        in_specs=[pl.BlockSpec(memory_space=pltpu.HBM)] * INPUTS,
        out_specs=[vm] * 2,
        scratch_shapes=[pltpu.VMEM(a.shape, a.dtype) for a in operands]
        + [
            pltpu.VMEM((864, 256), BF16),
            pltpu.VMEM((1024, 256), F32),
            pltpu.VMEM((4, 9, 24, 256), F32),
            pltpu.VMEM((256, 432), BF16),
            pltpu.VMEM((256, 1024), BF16),
            pltpu.VMEM((128, 2048), BF16),
            pltpu.VMEM((128, 256), BF16),
            pltpu.VMEM((1024, 256), BF16),
            pltpu.VMEM((128, 256), BF16),
            pltpu.VMEM((256, 256), BF16),
            pltpu.VMEM((2048, 256), BF16),
            pltpu.VMEM((256, 256), BF16),
            pltpu.VMEM((9, 24, 128), F32),
            pltpu.VMEM((120, 128), F32),
            pltpu.VMEM((144, 16), F32),
            pltpu.VMEM((TILES, 8, 128), F32),
            pltpu.VMEM((count, 8, 128), F32),
            dma((INPUTS,)),
            dma((6,)),
            dma((6,)),
            dma((TILES,)),
            dma,
            dma,
            dma((2,)),
        ],
        compiler_params=pltpu.CompilerParams(
            collective_id=0, has_side_effects=True, vmem_limit_bytes=62 * 1024 * 1024),
        cost_estimate=pl.CostEstimate(flops=10**9, bytes_accessed=2 * 10**6, transcendentals=3 * 10**5),
    )(*operands)
    out, gw2, gw1, gb1, gb2 = pl.pallas_call(
        unpack,
        out_shape=[
            jax.ShapeDtypeStruct((64, 128), BF16),
            jax.ShapeDtypeStruct((432, 32), F32),
            jax.ShapeDtypeStruct((27, 4, 16), F32),
            jax.ShapeDtypeStruct((1, 16), F32),
            jax.ShapeDtypeStruct((1, 32), F32),
        ],
        in_specs=[vm] * 2,
        out_specs=[vm] * 5,
        scratch_shapes=[pltpu.VMEM((112, 128), F32)],

    )(out, total)
    grad_w1 = jnp.transpose(gw1.reshape(3, 3, 3, 4, 16), (4, 3, 0, 1, 2))
    grad_w2 = jnp.transpose(gw2.reshape(3, 3, 3, 16, 32), (4, 3, 0, 1, 2))
    return out.reshape(1, 32, 1, 2, 128), grad_w1, gb1.reshape(16), grad_w2, gb2.reshape(32)


def solution(mesh):
    placed = (
        P("dp", None, "space", None, None),
        P("dp", None, "space", None, None),
        P(),
        P(),
        P(),
        P(),
    )
    return jax.shard_map(
        functools.partial(shards, mesh.shape["dp"], mesh.shape["space"]),
        mesh=mesh,
        in_specs=placed,
        out_specs=(P("dp", None, "space", None, None), P(), P(), P(), P()),
        check_vma=False,
    )
```

```python
import functools

import jax
import jax.numpy as jnp
import ml_dtypes
import numpy as np
from jax import lax
from jax.experimental import pallas as pl
from jax.experimental.pallas import tpu as pltpu
from jax.sharding import PartitionSpec as P

F32, BF16 = jnp.float32, jnp.bfloat16
MESH = pl.DeviceIdType.MESH
INPUTS = 11
EARLY, LATE = 128, 16


def dot(a, b, over=(1, 0)):
    return lax.dot_general(a, b, (((over[0],), (over[1],)), ((), ())), preferred_element_type=F32)


def sigmoid(v):
    return 0.5 * jnp.tanh(0.5 * v) + 0.5


def lanes(rows, width=128):
    return lax.broadcasted_iota(jnp.int32, (rows, width), 1)


def column(row, n):
    at = lax.broadcasted_iota(jnp.int32, (n, n), 0)
    return jnp.sum(jnp.where(at == lanes(n, n), row, 0.0), axis=1, keepdims=True)


def as_row(col, n):
    at = lax.broadcasted_iota(jnp.int32, (n, 128), 0)
    return jnp.sum(jnp.where(at == lanes(n), col, 0.0), axis=0, keepdims=True)


def spread(plane, ch, dst, base):
    lane = lanes(ch)
    zero = jnp.zeros((ch, 128), F32)
    src = {}
    for row in range(2):
        for u in range(2):
            for col in range(2):
                at = (row * 2 + col) * ch
                src[row, u, col] = plane[at : at + ch, u * 128 : u * 128 + 128].astype(F32)
            src[row, u, -1] = jnp.where(lane == 0, 0.0, pltpu.roll(src[row, u, 1], 1, 1))
            src[row, u, 2] = jnp.where(lane == 127, 0.0, pltpu.roll(src[row, u, 0], 127, 1))
    for row in range(-1, 3):
        for col in range(-1, 3):
            at = base + ((row + 1) * 4 + col + 1) * ch
            if row == -1:
                pair = (zero, src[1, 0, col])
            elif row == 2:
                pair = (src[0, 1, col], zero)
            else:
                pair = (src[row, 0, col], src[row, 1, col])
            dst[at : at + ch, 0:128] = pair[0].astype(BF16)
            dst[at : at + ch, 128:256] = pair[1].astype(BF16)


def kernel(
    nd, ns,
    *refs,
):
    hbm, (out, total, late) = refs[:INPUTS], refs[INPUTS : INPUTS + 3]
    held, refs = refs[INPUTS + 3 : 2 * INPUTS + 3], refs[2 * INPUTS + 3 :]
    vol, cot, w1, b1, w2, b2, pmat, emat, rep1, rep2, operm = held
    (
    field, slope1, taps, w1t, w2t, wback, pool, poolx, phalo, grad, gradx, ghalo, fold_a, fold_b,
    w1_rows, sums, near, far, late_near, late_far, load_sem, send_sem, recv_sem, near_sem, far_sem,
    ) = refs
    dp, sp = lax.axis_index("dp"), lax.axis_index("space")
    has_left, has_right = sp > 0, sp < ns - 1

    barrier = pltpu.get_barrier_semaphore()

    def beside(k):
        return (dp, lax.rem(sp + k, ns))

    def across(k):
        return (lax.rem(dp + k, nd), sp)

    def greet(target):
        def step(k, carry):
            pl.semaphore_signal(barrier, inc=1, device_id=target(k), device_id_type=MESH)
            return carry
        return step

    lax.fori_loop(1, ns, greet(beside), 0)
    lax.fori_loop(1, nd, greet(across), 0)
    loads = [pltpu.make_async_copy(hbm[i], held[i], load_sem.at[i]) for i in range(INPUTS)]
    for copy in loads:
        copy.start()

    class Exchange:
        def __init__(self, slot, to_left, to_right, from_left, from_right):
            self.left = lambda: pltpu.make_async_remote_copy(
                src_ref=to_left, dst_ref=from_right, send_sem=send_sem.at[2 * slot],
                recv_sem=recv_sem.at[2 * slot], device_id=(dp, sp - 1), device_id_type=MESH)
            self.right = lambda: pltpu.make_async_remote_copy(
                src_ref=to_right, dst_ref=from_left, send_sem=send_sem.at[2 * slot + 1],
                recv_sem=recv_sem.at[2 * slot + 1], device_id=(dp, sp + 1), device_id_type=MESH)
            self.from_left, self.from_right = from_left, from_right

        def start(self):
            @pl.when(has_left)
            def _():
                self.left().start()

            @pl.when(has_right)
            def _():
                self.right().start()

        def receive(self):
            @pl.when(has_left)
            def _():
                self.right().wait_recv()

            @pl.when(has_right)
            def _():
                self.left().wait_recv()

        def clear(self):
            @pl.when(jnp.logical_not(has_left))
            def _():
                self.from_left[...] = jnp.zeros(self.from_left.shape, BF16)

            @pl.when(jnp.logical_not(has_right))
            def _():
                self.from_right[...] = jnp.zeros(self.from_right.shape, BF16)

        def finish(self):
            @pl.when(has_left)
            def _():
                self.left().wait_send()

            @pl.when(has_right)
            def _():
                self.right().wait_send()

    rows = lambda ref, at, n: ref.at[pl.ds(at, n)]
    ex_field = Exchange(0, rows(field, 144, 144), rows(field, 576, 144), rows(field, 0, 144), rows(field, 720, 144))
    ex_pool = Exchange(1, rows(pool, 0, 64), rows(pool, 64, 64), rows(phalo, 0, 64), rows(phalo, 64, 64))
    ex_grad = Exchange(2, rows(grad, 0, 128), rows(grad, 128, 128), rows(ghalo, 0, 128), rows(ghalo, 128, 128))

    first_used = (0, 6, 7)
    for i in first_used:
        loads[i].wait()
    phases = dot(vol[...], pmat[...])
    part = [phases[:, q * 128 : q * 128 + 128] for q in range(4)]
    lane = lanes(128)
    before = jnp.where(lane == 0, 0.0, pltpu.roll(part[3], 1, 1))
    after = jnp.where(lane == 127, 0.0, pltpu.roll(part[0], 127, 1))
    part = [before] + part + [after]
    stacked = jnp.concatenate(
        [
            jnp.concatenate(
                [part[q][(c * 4 + x) * 8 : (c * 4 + x) * 8 + 8] for q in range(6) for c in range(4)], axis=0)
            for x in range(4)
        ],
        axis=1,
    ).astype(BF16)
    blocks = dot(emat[...], stacked).astype(BF16)
    for x in range(4):
        for u in range(2):
            field[144 * (x + 1) : 144 * (x + 2), u * 128 : u * 128 + 128] = blocks[
                u * 144 : u * 144 + 144, x * 128 : x * 128 + 128]

    pl.semaphore_wait(barrier, ns + nd - 2)
    ex_field.start()
    ex_field.clear()
    ex_pool.clear()
    ex_grad.clear()

    for i in range(INPUTS):
        if i not in first_used:
            loads[i].wait()

    wide = lanes(24, 256)
    w1_rows[...] = jnp.zeros(w1_rows.shape, F32)
    for k in range(27):
        at = 16 * (k // 3) + 4 * (k % 3)
        w1_rows[at : at + 4, :] = w1[k].astype(F32)
    rep = dot(w1_rows[...].astype(BF16), rep1[...])
    taps[...] = jnp.zeros(taps.shape, F32)
    for q in range(4):
        for k in range(9):
            taps[q, k, 4 * q : 4 * q + 12, :] = rep[16 * k : 16 * k + 12]
    in_q = [lax.rem(wide // 16, 4) == q for q in range(4)]
    in_r = [wide // 64 == r for r in range(4)]
    band = []
    for k in range(9):
        blk = taps[0, k]
        for q in range(1, 4):
            blk = jnp.where(in_q[q], taps[q, k], blk)
        band.append(blk)
    rows_out = []
    for a in range(3):
        for y in range(6):
            blk = jnp.zeros((24, 256), F32)
            for r in range(4):
                if 0 <= y - r <= 2:
                    blk = jnp.where(in_r[r], band[a * 3 + y - r], blk)
            rows_out.append(blk)
    w1t[...] = jnp.concatenate(rows_out, axis=0).T.astype(BF16)

    bias1 = jnp.concatenate([column(b1[...], 16)] * 16, axis=0)
    bias2 = jnp.concatenate([column(b2[...], 32)] * 8, axis=0)
    acts = {}

    def first(i):
        v = dot(w1t[...], field[144 * i : 144 * i + 432]) + bias1
        s = sigmoid(v)
        slope1[256 * i : 256 * i + 256] = 0.125 * (s * (1.0 + v * (1.0 - s)))
        acts[i] = v * s

    first(1)
    first(2)

    rep = dot(w2[...], rep2[...])
    tap = lambda a, b, e: rep[((a * 3 + b) * 3 + e) * 16 : ((a * 3 + b) * 3 + e) * 16 + 16]
    own = lanes(16, 256) // 32
    rows_out = []
    for pi in range(4):
        for pr in range(4):
            for pq in range(4):
                blk = jnp.zeros((16, 256), F32)
                for k in range(8):
                    a, b, e = pi - k // 4, pr - (k // 2) % 2, pq - k % 2
                    if 0 <= a <= 2 and 0 <= b <= 2 and 0 <= e <= 2:
                        blk = jnp.where(own == k, tap(a, b, e), blk)
                rows_out.append(blk)
    w2t[...] = jnp.concatenate(rows_out, axis=0).T.astype(BF16)
    quarter = lanes(16) // 32
    back_tap = {}
    for a in range(3):
        for b in range(3):
            for col in range(2):
                blk = jnp.zeros((16, 128), F32)
                for e in range(3):
                    blk = jnp.where(quarter == col + 2 - e, tap(a, b, e)[:, 0:128], blk)
                back_tap[a, b, col] = blk.astype(BF16)
    none = jnp.zeros((16, 128), BF16)
    for k in range(8):
        for pi in range(4):
            for pr in range(4):
                at = (pi * 4 + pr) * 128
                wback[16 * k : 16 * k + 16, at : at + 128] = back_tap.get(
                    (k // 4 + 2 - pi, (k // 2) % 2 + 2 - pr, k % 2), none)

    ex_field.receive()
    first(0)
    first(3)
    for i in range(2):
        both = acts[2 * i] + acts[2 * i + 1]
        for row in range(2):
            for col in range(2):
                blk = 0.0
                for r in range(2 * row, 2 * row + 2):
                    for q in range(2 * col, 2 * col + 2):
                        blk = blk + both[(r * 4 + q) * 16 : (r * 4 + q) * 16 + 16]
                at = 64 * i + (row * 2 + col) * 16
                pool[at : at + 16] = (blk * 0.125).astype(BF16)
    ex_pool.start()
    spread(pool[0:64], 16, poolx, 256)
    spread(pool[64:128], 16, poolx, 512)
    v = dot(w2t[:, 256:768], poolx[256:768])
    cot_cols = dot(operm[...], cot[...])
    cot_cols = jnp.concatenate([cot_cols[0:32], cot_cols[32:64]], axis=1) * 0.125
    ex_pool.receive()
    spread(phalo[0:64], 16, poolx, 0)
    spread(phalo[64:128], 16, poolx, 768)
    v = v + dot(w2t[:, 0:256], poolx[0:256]) + dot(w2t[:, 768:1024], poolx[768:1024]) + bias2
    s = sigmoid(v)
    act = v * s
    slope = s * (1.0 + v * (1.0 - s))
    out_sum, grad_sum = 0.0, 0.0
    for k in range(8):
        blk = (cot_cols * slope[32 * k : 32 * k + 32]).astype(BF16)
        grad[32 * k : 32 * k + 32] = blk
        grad_sum = grad_sum + blk.astype(F32)
        out_sum = out_sum + act[32 * k : 32 * k + 32]
    ex_grad.start()

    prod = dot(poolx[...], grad[...], (1, 1))
    packed = [jnp.zeros((16, 128), F32) for _ in range(7)]
    for a in range(3):
        for b in range(3):
            for e in range(3):
                blk = jnp.zeros((16, 256), F32)
                for k in range(8):
                    at = (((k // 4 + a) * 4 + (k // 2) % 2 + b) * 4 + k % 2 + e) * 16
                    blk = jnp.where(own == k, prod[at : at + 16], blk)
                half = blk[:, 0:128] + blk[:, 128:256]
                half = half + pltpu.roll(half, 64, 1)
                half = half + pltpu.roll(half, 32, 1)
                at = (a * 3 + b) * 3 + e
                packed[at % 7] = jnp.where(quarter == at // 7, half, packed[at % 7])
    row2 = as_row(jnp.sum(grad_sum, axis=1, keepdims=True), 32)
    packed.append(jnp.where(lax.broadcasted_iota(jnp.int32, (16, 128), 0) == 0, row2, 0.0))
    sums[...] = jnp.concatenate(packed, axis=0).reshape(sums.shape)

    class Step:
        def __init__(self, src, dst, slot, target, size, send, recv):
            def copy(k):
                return pltpu.make_async_remote_copy(
                    src_ref=src(k), dst_ref=dst.at[slot], send_sem=send, recv_sem=recv,
                    device_id=target(k), device_id_type=MESH)

            self.copy, self.all, self.size, self.send, self.recv = copy, dst, size, send, recv

        def start(self):
            def step(k, carry):
                self.copy(k).start()
                return carry

            lax.fori_loop(1, self.size, step, 0)

        def wait(self, sem):
            others = self.all.at[pl.ds(0, self.size - 1)]
            pltpu.make_async_copy(others, others, sem).wait()

        def receive(self):
            self.wait(self.recv)

        def finish(self):
            self.wait(self.send)

    spread_out = Step(lambda k: sums.at[lax.rem(sp + k, ns)], near, sp, beside, ns, near_sem.at[0], near_sem.at[1])
    sum_far = Step(lambda k: far.at[dp], far, dp, across, nd, far_sem.at[0], far_sem.at[1])
    collect = Step(lambda k: total.at[sp], total, sp, beside, ns, near_sem.at[2], near_sem.at[3])
    small_near = Step(lambda k: late_near.at[sp], late_near, sp, beside, ns, near_sem.at[4], near_sem.at[5])
    small_far = Step(lambda k: late_far.at[dp], late_far, dp, across, nd, far_sem.at[2], far_sem.at[3])
    spread_out.start()
    near[sp] = sums[sp]

    res = (out_sum * 0.125).astype(BF16)
    res = jnp.concatenate([res[:, 0:128], res[:, 128:256]], axis=0)
    out[...] = dot(operm[...], res, (0, 0)).astype(BF16)

    spread(grad[0:128], 32, gradx, 512)
    spread(grad[128:256], 32, gradx, 1024)
    back = dot(wback[:, 512:1536], gradx[512:1536])
    ex_grad.receive()
    spread(ghalo[0:128], 32, gradx, 0)
    spread(ghalo[128:256], 32, gradx, 1536)
    back = back + dot(wback[:, 0:512], gradx[0:512]) + dot(wback[:, 1536:2048], gradx[1536:2048])

    spread_out.receive()
    far[dp] = jnp.sum(near[...], axis=0)
    sum_far.start()
    prod = jnp.zeros((432, 256), F32)
    bias_sum = jnp.zeros((16, 256), F32)
    for i in range(4):
        blks = []
        for r in range(4):
            for q in range(4):
                at = (((i // 2) * 2 + r // 2) * 2 + q // 2) * 16
                k = 256 * i + (r * 4 + q) * 16
                blk = (back[at : at + 16] * slope1[k : k + 16]).astype(BF16)
                bias_sum = bias_sum + blk.astype(F32)
                blks.append(blk)
        prod = prod + dot(field[144 * i : 144 * i + 432], jnp.concatenate(blks, axis=0), (1, 1))

    for a in range(3):
        for b in range(3):
            blk = jnp.zeros((24, 256), F32)
            for r in range(4):
                at = (a * 6 + r + b) * 24
                blk = jnp.where(in_r[r], prod[at : at + 24], blk)
            half = blk[:, 0:128] + blk[:, 128:256]
            fold_a[a * 3 + b] = half + pltpu.roll(half, 64, 1)
    sixteenth = lanes(12) // 16
    for k in range(9):
        blk = jnp.zeros((12, 128), F32)
        for q in range(4):
            blk = jnp.where(lax.rem(sixteenth, 4) == q, fold_a[k, 4 * q : 4 * q + 12, :], blk)
        blk = blk + pltpu.roll(blk, 32, 1)
        blk = blk + pltpu.roll(blk, 16, 1)
        fold_b[12 * k : 12 * k + 12, :] = blk
    fold_b[108:120, :] = jnp.zeros((12, 128), F32)
    blk = fold_b[0:16]
    for g in range(1, 8):
        blk = jnp.where(lanes(16) // 16 == g, fold_b[14 * g : 14 * g + 16, :], blk)
    at = lax.broadcasted_iota(jnp.int32, (16, 128), 0)
    row1 = as_row(jnp.sum(bias_sum, axis=1, keepdims=True), 16)
    late_near[sp] = jnp.where(at == 14, row1, jnp.where(at == 15, 0.0, blk))
    small_near.start()
    small_near.receive()
    late_far[dp] = jnp.sum(late_near[...], axis=0)
    small_far.start()
    sum_far.receive()
    total[sp] = jnp.sum(far[...], axis=0)
    collect.start()
    collect.receive()
    small_far.receive()
    late[...] = jnp.sum(late_far[...], axis=0)

    ex_field.finish()
    ex_pool.finish()
    ex_grad.finish()

    for step in (spread_out, sum_far, collect, small_near, small_far):
        step.finish()


def unpack(res, total, late, out, gw2, gw1, gb1, gb2, rows):
    out[...] = res[...]
    for g in range(4):
        n = 112 if g < 3 else 96
        blk = total[0:n]
        if g:
            blk = pltpu.roll(blk, 128 - 32 * g, 1)
        gw2[112 * g : 112 * g + n] = blk[:, 0:32]
    blk = late[...]
    for g in range(8):
        n = 14 if g < 7 else 10
        turned = pltpu.roll(blk, 128 - 16 * g, 1) if g else blk
        rows[14 * g : 14 * g + n] = turned[0:n]
    for k in range(27):
        gw1[k] = rows[4 * k : 4 * k + 4, 0:16]
    gb1[...] = blk[14:15, 0:16]
    gb2[...] = total[112:113, 0:32]


def tables():
    pmat = np.zeros((512, 512), np.float32)
    for z in range(512):
        pmat[z, (z % 4) * 128 + z // 4] = 1
    emat = np.zeros((2, 6, 6, 4, 6, 4, 8), np.float32)
    for u in range(2):
        for yr in range(6):
            y = 4 * u + yr - 1
            if 0 <= y < 8:
                for q in range(6):
                    for c in range(4):
                        emat[u, yr, q, c, q, c, y] = 1
    rep1 = np.tile(np.eye(16, dtype=np.float32), (1, 16))
    rep2 = np.tile(np.eye(32, dtype=np.float32), (1, 8))
    operm = np.zeros((64, 64), np.float32)
    for u in range(2):
        for o in range(32):
            operm[u * 32 + o, o * 2 + u] = 1
    return [t.astype(ml_dtypes.bfloat16) for t in (pmat, emat.reshape(288, 192), rep1, rep2, operm)]


def shards(nd, ns, volume, cotangent, w_first, b_first, w_second, b_second):
    each = EARLY // ns
    w1 = jnp.transpose(w_first, (2, 3, 4, 1, 0)).reshape(27, 4, 16)
    w2 = jnp.transpose(w_second, (2, 3, 4, 1, 0)).reshape(432, 32)
    vm = pl.BlockSpec(memory_space=pltpu.VMEM)
    dma = pltpu.SemaphoreType.DMA
    operands = [
        volume.reshape(128, 512), cotangent.reshape(64, 128), w1, b_first.reshape(1, 16), w2,
        b_second.reshape(1, 32), *tables(),
    ]
    out, total, late = pl.pallas_call(
        functools.partial(kernel, nd, ns),
        out_shape=[
            jax.ShapeDtypeStruct((64, 128), BF16),
            jax.ShapeDtypeStruct((ns, each, 128), F32),
            jax.ShapeDtypeStruct((LATE, 128), F32),
        ],
        in_specs=[pl.BlockSpec(memory_space=pltpu.HBM)] * INPUTS,
        out_specs=[vm] * 3,
        scratch_shapes=[pltpu.VMEM(a.shape, a.dtype) for a in operands]
        + [
            pltpu.VMEM((864, 256), BF16),
            pltpu.VMEM((1024, 256), F32),
            pltpu.VMEM((4, 9, 24, 256), F32),
            pltpu.VMEM((256, 432), BF16),
            pltpu.VMEM((256, 1024), BF16),
            pltpu.VMEM((128, 2048), BF16),
            pltpu.VMEM((128, 256), BF16),
            pltpu.VMEM((1024, 256), BF16),
            pltpu.VMEM((128, 256), BF16),
            pltpu.VMEM((256, 256), BF16),
            pltpu.VMEM((2048, 256), BF16),
            pltpu.VMEM((256, 256), BF16),
            pltpu.VMEM((9, 24, 128), F32),
            pltpu.VMEM((120, 128), F32),
            pltpu.VMEM((144, 16), F32),
            pltpu.VMEM((ns, each, 128), F32),
            pltpu.VMEM((ns, each, 128), F32),
            pltpu.VMEM((nd, each, 128), F32),
            pltpu.VMEM((ns, LATE, 128), F32),
            pltpu.VMEM((nd, LATE, 128), F32),
            dma((INPUTS,)),
            dma((6,)),
            dma((6,)),
            dma((6,)),
            dma((4,)),
        ],
        compiler_params=pltpu.CompilerParams(
            collective_id=0, has_side_effects=True, vmem_limit_bytes=62 * 1024 * 1024),
        cost_estimate=pl.CostEstimate(flops=10**9, bytes_accessed=2 * 10**6, transcendentals=3 * 10**5),
    )(*operands)
    out, gw2, gw1, gb1, gb2 = pl.pallas_call(
        unpack,
        out_shape=[
            jax.ShapeDtypeStruct((64, 128), BF16),
            jax.ShapeDtypeStruct((432, 32), F32),
            jax.ShapeDtypeStruct((27, 4, 16), F32),
            jax.ShapeDtypeStruct((1, 16), F32),
            jax.ShapeDtypeStruct((1, 32), F32),
        ],
        in_specs=[vm] * 3,
        out_specs=[vm] * 5,
        scratch_shapes=[pltpu.VMEM((112, 128), F32)],

    )(out, total.reshape(EARLY, 128), late)
    grad_w1 = jnp.transpose(gw1.reshape(3, 3, 3, 4, 16), (4, 3, 0, 1, 2))
    grad_w2 = jnp.transpose(gw2.reshape(3, 3, 3, 16, 32), (4, 3, 0, 1, 2))
    return out.reshape(1, 32, 1, 2, 128), grad_w1, gb1.reshape(16), grad_w2, gb2.reshape(32)


def solution(mesh):
    placed = (
        P("dp", None, "space", None, None),
        P("dp", None, "space", None, None),
        P(),
        P(),
        P(),
        P(),
    )
    return jax.shard_map(
        functools.partial(shards, mesh.shape["dp"], mesh.shape["space"]),
        mesh=mesh,
        in_specs=placed,
        out_specs=(P("dp", None, "space", None, None), P(), P(), P(), P()),
        check_vma=False,
    )
```
